32 devices in a mesh: groups: 2 (over x), traj: 16 (over z, y, core).
Axes of the slice: x: 2, y: 2, z: 4, core: 2. Of those that a mesh axis runs over, the one named last changes fastest.
Arguments:
- lengths: int32 [8], P('groups'), parts along dimension 0, may hold values from 1 to 4096, 8192 in all
- pattern: int32 [8, 8], replicated, may hold values from 0 to 31, as said below
- first_blocks: bfloat16 [8192, 128], replicated, may hold values from -0.1875 to 0.1875
- second_weight: bfloat16 [1024, 512], replicated, may hold values from -0.1875 to 0.1875
- frames: bfloat16 [16384, 4096], P(('groups', 'traj')), parts along dimension 0, may hold values from -14 to 14
- frame_ok: int32 [16384], P(('groups', 'traj')), parts along dimension 0, may hold values 0 or 1
Outputs:
- score: float32 [2], P('groups'), parts along dimension 0
- grad_first: float32 [16384, 128], P(('groups', 'traj')), parts along dimension 0
- grad_second: float32 [2048, 512], P(('groups', 'traj')), parts along dimension 0
The draws below stay inside these ranges and needn't reach their ends.
There are 2 independent parts, one for each index of `groups`. The reference program is written for one: setup_inputs(seed, part) draws one part's arguments, and reference() takes and returns one part's arrays. A program takes and returns all parts, laid end to end along the dimension named above; an argument that names none is the same for every part. Nothing has to cross between parts.
Inputs may be any that keep to these rules, and one draw needn't show every extreme that they name: `lengths`: the longest trajectory has exactly 4096 frames. `pattern`: indices are distinct within a column block and every row block appears somewhere.
All inputs are finite; a program needn't handle non-finite values. No bound on the sum of `frame_ok` on one device may be relied on, other than what follows from the above.
Results may differ from the reference program's by a relative error of at most 0.013.
Values may be sent and summed in bfloat16 or wider, within the bound.
A program may use at most 128 MiB of HBM per device.

```python
import math
import jax
import jax.numpy as jnp
import numpy as np
from jax import lax

F = 4096
HID = 1024
OUT = 512
BLK = 128
KB = 8
LAG = 64
SEG = 512
NRB = 32
NCB = 8
TOTAL = 8192
TRAJS = 4
N_TRAJ = 16


def draw_frames(key, part):
    key = jax.random.fold_in(key, 11)
    key_noise, key_slow = jax.random.split(key, 2)
    slow = jax.random.truncated_normal(key_slow, -4.0, 4.0, (TOTAL // LAG + 1, F), jnp.float32)
    index = jnp.arange(TOTAL, dtype=jnp.int32) // LAG
    noise = jax.random.truncated_normal(key_noise, -4.0, 4.0, (TOTAL, F), jnp.float32)
    values = 0.6 * noise + 0.55 * (slow[index] + slow[index + 1])
    return values.astype(jnp.bfloat16)


def draw_pattern(key, part):
    key = jax.random.fold_in(key, 23)
    copies = NCB * KB // NRB
    keys = jax.random.split(key, copies)
    orders = jax.vmap(lambda single: jax.random.permutation(single, NRB))(keys)
    return orders.reshape(NCB, KB).astype(jnp.int32)


def place_ends(entries, own_key, least, top_value):
    extent = entries.shape
    index_at = [jax.random.randint(jax.random.fold_in(own_key, axis), (), 0, extent[axis]) for axis in range(len(extent))]
    entries = entries.at[tuple(index_at)].set(least)
    longest = extent.index(max(extent))
    index_at[longest] = (index_at[longest] + 1) % extent[longest]
    return entries.at[tuple(index_at)].set(top_value)


def profile(count, total, reach, skew):
    weights = [(1 << 20) // math.isqrt(grade ** skew) + 1 for grade in range(2, count + 1)]
    spare, given = total - reach - (count - 1), [1] * (count - 1)
    while spare > 0:
        candidates = [i for i in range(count - 1) if given[i] < reach]
        mass, budget = sum([weights[i] for i in candidates]), spare
        for i in candidates:
            more = min(reach - given[i], max(1, budget * weights[i] // mass), spare)
            given[i] = given[i] + more
            spare = spare - more
    return np.array([reach] + given)


def ragged(stream_key, amount, total, most, skew):
    if amount == 2:
        one = jax.random.randint(stream_key, (), max(1, total - most), min(most, total - 1) + 1)
        return jnp.stack([one, total - one])
    tallies = jnp.asarray(profile(amount, total, most, skew), jnp.int32)
    couples = (amount - 1) // 2
    giver, taker = tallies[1:1 + 2 * couples:2], tallies[2:2 + 2 * couples:2]
    slack = jnp.minimum(giver - 1, most - taker)
    passed = jax.random.randint(jax.random.fold_in(stream_key, 1), (couples,), 0, 1 << 20) % (slack + 1)
    tallies = tallies.at[1:1 + 2 * couples:2].set(giver - passed).at[2:2 + 2 * couples:2].set(taker + passed)
    return tallies[jax.random.permutation(jax.random.fold_in(stream_key, 2), amount)]


def gaussian(key, extent, spread, most, kind=jnp.bfloat16):
    result = spread * jax.random.normal(key, extent, jnp.float32)
    return jnp.clip(result, min=-most, max=most).astype(kind)


def setup_inputs(seed: int = 0, part: int = 0) -> dict:
    key_list = jax.random.split(jax.random.key(seed), 7)
    own_keys = jax.random.split(jax.random.fold_in(key_list[6], part), 7)
    lengths = ragged(own_keys[0], TRAJS, TOTAL, 8 * SEG, 2).astype(jnp.int32)
    pattern = draw_pattern(jax.random.fold_in(key_list[6], 71), part)
    first_blocks = gaussian(key_list[2], (NCB * KB * BLK, BLK), (KB * BLK) ** -0.5, 0.1875)
    second_weight = gaussian(key_list[3], (HID, OUT), HID ** -0.5, 0.1875)
    frames = draw_frames(jax.random.fold_in(jax.random.fold_in(key_list[6], part), 71), part)
    frame_ok = place_ends((jax.random.randint(own_keys[5], (TOTAL,), 0, 8) < 7).astype(jnp.int32), jax.random.fold_in(own_keys[5], 1), 0, 1)
    return {"lengths": lengths, "pattern": pattern, "first_blocks": first_blocks, "second_weight": second_weight, "frames": frames, "frame_ok": frame_ok}


EPS = 0.01

def vamp_score(weight_sum, sum_a, sum_b, mom_aa, mom_ab, mom_bb):
    mean_a = sum_a / weight_sum
    mean_b = sum_b / weight_sum
    identity = jnp.eye(mom_aa.shape[0], dtype=mom_aa.dtype)
    cov_aa = mom_aa / weight_sum - jnp.outer(mean_a, mean_a) + EPS * identity
    cov_bb = mom_bb / weight_sum - jnp.outer(mean_b, mean_b) + EPS * identity
    cov_ab = mom_ab / weight_sum - jnp.outer(mean_a, mean_b)
    factor_a = jnp.linalg.cholesky(cov_aa)
    factor_b = jnp.linalg.cholesky(cov_bb)
    partial_solve = jax.scipy.linalg.solve_triangular(factor_a, cov_ab, lower=True)
    whitened = jax.scipy.linalg.solve_triangular(factor_b, partial_solve.T, lower=True)
    return jnp.sum(whitened * whitened) / mom_aa.shape[0]

def pair_weights(lengths, ok_now, ok_lagged, offset):
    positions = offset + jnp.arange(ok_now.shape[0], dtype=jnp.int32)
    bounds = jnp.cumsum(lengths).astype(jnp.int32)
    owner_now = lax.optimization_barrier(jnp.sum((bounds[None, :] <= positions[:, None]).astype(jnp.int32), axis=1))
    owner_lag = lax.optimization_barrier(jnp.sum((bounds[None, :] <= (positions + LAG)[:, None]).astype(jnp.int32), axis=1))
    keep = (owner_now == owner_lag) & (ok_now > 0.5) & (ok_lagged > 0.5)
    return keep.astype(jnp.float32)

def pick_blocks(rows, pattern):
    split_rows = rows.reshape(rows.shape[0], rows.shape[1] // BLK, BLK)
    return split_rows[:, pattern]

def encode(rows, pattern, first_blocks, second_weight):
    picked = pick_blocks(rows, pattern)
    blocks = first_blocks.reshape(pattern.shape[0], pattern.shape[1], BLK, BLK)
    pre = jnp.einsum('rckb,ckbd->rcd', picked.astype(jnp.float32), blocks.astype(jnp.float32))
    squash = jnp.tanh(pre.reshape(rows.shape[0], -1))
    hidden = squash.astype(jnp.bfloat16)
    codes = jnp.dot(hidden.astype(jnp.float32), second_weight.astype(jnp.float32), preferred_element_type=jnp.float32)
    return (squash, hidden, codes)

def moments(weights, codes_a, codes_b):
    highest = lax.Precision.HIGHEST
    contract = (((0,), (0,)), ((), ()))
    scaled_a = codes_a * weights[:, None]
    scaled_b = codes_b * weights[:, None]
    return (jnp.sum(weights), lax.optimization_barrier(jnp.sum(scaled_a, axis=0)), lax.optimization_barrier(jnp.sum(scaled_b, axis=0)), lax.dot_general(scaled_a, codes_a, contract, precision=highest), lax.dot_general(scaled_a, codes_b, contract, precision=highest), lax.dot_general(scaled_b, codes_b, contract, precision=highest))

def code_cotangents(weights, codes_a, codes_b, grads):
    highest = lax.Precision.HIGHEST
    g_sa, g_sb, g_aa, g_ab, g_bb = (grads[1], grads[2], grads[3], grads[4], grads[5])
    cot_a = weights[:, None] * (g_sa[None, :] + jnp.dot(codes_a, g_aa + g_aa.T, precision=highest) + jnp.dot(codes_b, g_ab.T, precision=highest))
    cot_b = weights[:, None] * (g_sb[None, :] + jnp.dot(codes_b, g_bb + g_bb.T, precision=highest) + jnp.dot(codes_a, g_ab, precision=highest))
    return (cot_a.astype(jnp.bfloat16), cot_b.astype(jnp.bfloat16))

def role_terms(picked, squash, hidden, cotan, second_weight):
    back_hidden = lax.dot_general(cotan.astype(jnp.float32), second_weight.astype(jnp.float32), (((1,), (1,)), ((), ())), preferred_element_type=jnp.float32)
    back_pre = (back_hidden * (1.0 - squash * squash)).astype(jnp.bfloat16)
    grad_second = lax.dot_general(hidden.astype(jnp.float32), cotan.astype(jnp.float32), (((0,), (0,)), ((), ())), preferred_element_type=jnp.float32)
    back_split = back_pre.reshape(back_pre.shape[0], picked.shape[1], BLK)
    grad_first = jnp.einsum('rckb,rcd->ckbd', picked.astype(jnp.float32), back_split.astype(jnp.float32))
    return (grad_first, grad_second)

def reference(lengths, pattern, first_blocks, second_weight, frames, frame_ok):
    total_rows = frames.shape[0]
    blocked = frames.reshape(N_TRAJ, SEG, frames.shape[1])

    def forward(block):
        return encode(block, pattern, first_blocks, second_weight)
    squash, hidden, codes = lax.map(forward, blocked)
    codes = codes.reshape(total_rows, -1)
    codes_b = jnp.concatenate([codes[LAG:], jnp.zeros((LAG, codes.shape[1]), jnp.float32)], axis=0)
    ok_lagged = jnp.concatenate([frame_ok[LAG:], jnp.zeros((LAG,), jnp.int32)], axis=0)
    weights = pair_weights(lengths, frame_ok, ok_lagged, 0)
    stats = moments(weights, codes, codes_b)
    score, pull = jax.vjp(vamp_score, *stats)
    grads = pull(jnp.ones_like(score))
    cot_a, cot_b = code_cotangents(weights, codes, codes_b, grads)
    cot_shifted = jnp.concatenate([jnp.zeros((LAG, cot_b.shape[1]), jnp.bfloat16), cot_b[:total_rows - LAG]], axis=0)
    frame_cot = (cot_a.astype(jnp.float32) + cot_shifted.astype(jnp.float32)).astype(jnp.bfloat16)
    width = codes.shape[1]

    def accumulate(carry, items):
        block, squash_blk, hidden_blk, cot_blk = items
        picked = pick_blocks(block, pattern)
        first_t, second_t = role_terms(picked, squash_blk, hidden_blk, cot_blk, second_weight)
        return ((carry[0] + first_t, carry[1] + second_t), None)
    start = (jnp.zeros((pattern.shape[0], pattern.shape[1], BLK, BLK), jnp.float32), jnp.zeros((second_weight.shape[0], width), jnp.float32))
    items = (blocked, squash, hidden, frame_cot.reshape(N_TRAJ, SEG, width))
    totals, unused = lax.scan(accumulate, start, items)
    grad_first = totals[0].reshape(-1, BLK)
    return (score.reshape(1), grad_first, totals[1])
```

```python
import functools

import jax
import jax.numpy as jnp
from jax import lax
from jax.experimental import pallas as pl
from jax.experimental.pallas import tpu as pltpu
from jax.sharding import PartitionSpec as P

BLK = 128
LAG = 64
EPS = 0.01
HIGHEST = lax.Precision.HIGHEST
VMEM = pl.BlockSpec(memory_space=pltpu.VMEM)
SMEM = pl.BlockSpec(memory_space=pltpu.SMEM)
LIMIT = 50 * 1024 * 1024


def from_behind(block, axis, distance):
    devices = range(lax.axis_size(axis))
    route = [(i - distance, i) for i in devices if i - distance in devices]
    return lax.ppermute(block, axis, route)


def pair_weights(lengths, ok_now, ok_lagged, offset):
    positions = offset + jnp.arange(ok_now.shape[0], dtype=jnp.int32)
    bounds = jnp.cumsum(lengths)
    owner_now = jnp.sum((bounds[None, :] <= positions[:, None]).astype(jnp.int32), axis=1)
    owner_lag = jnp.sum((bounds[None, :] <= (positions + LAG)[:, None]).astype(jnp.int32), axis=1)
    keep = (owner_now == owner_lag) & (ok_now > 0.5) & (ok_lagged > 0.5)
    return keep.astype(jnp.float32)


def mm(a, b, dims=((1,), (0,)), precision=HIGHEST):
    return lax.dot_general(
        a, b, (dims, ((), ())), precision=precision, preferred_element_type=jnp.float32
    )


def mm_bf16(a, b, dims=((1,), (0,))):
    return lax.dot_general(a, b, (dims, ((), ())), preferred_element_type=jnp.float32)


def split(x):
    high = x.astype(jnp.bfloat16)
    return high, (x - high.astype(jnp.float32)).astype(jnp.bfloat16)


def mm3(a, b, dims=((1,), (0,))):
    return mm_bf16(a[0], b[0], dims) + (mm_bf16(a[0], b[1], dims) + mm_bf16(a[1], b[0], dims))


def picked_columns(pattern_ref, frames_ref, col, slots):
    parts = []
    for slot in range(slots):
        start = pl.multiple_of(pattern_ref[col, slot] * BLK, BLK)
        parts.append(frames_ref[:, pl.ds(start, BLK)])
    return jnp.concatenate(parts, axis=1)


def encode_kernel(pattern_ref, frames_ref, first_ref, second_ref, squash_ref, hidden_ref, codes_ref):
    cols, slots = pattern_ref.shape
    depth = slots * BLK

    def column(col, _):
        picked = picked_columns(pattern_ref, frames_ref, col, slots)
        blocks = first_ref[pl.ds(pl.multiple_of(col * depth, depth), depth), :]
        squash = jnp.tanh(mm_bf16(picked, blocks))
        at = pl.ds(pl.multiple_of(col * BLK, BLK), BLK)
        squash_ref[:, at] = squash
        hidden_ref[:, at] = squash.astype(jnp.bfloat16)
        return 0

    lax.fori_loop(0, cols, column, 0)
    codes_ref[...] = mm_bf16(hidden_ref[...], second_ref[...])


def moments_kernel(codes_ref, far_ref, weights_ref, out_ref):
    codes = codes_ref[...]
    lagged = jnp.concatenate([codes[LAG:], far_ref[...].astype(jnp.float32)], axis=0)
    weights = weights_ref[...]
    scaled_a = codes * weights
    scaled_b = lagged * weights
    out = codes.shape[1]
    nb = out // BLK
    over_rows = ((0,), (0,))
    at = 0
    for left, right, whole in ((scaled_a, codes, False), (scaled_b, lagged, False), (scaled_a, lagged, True)):
        product = mm(left, right, over_rows)
        for i in range(nb):
            for j in range(0 if whole else i, nb):
                out_ref[pl.ds(at, BLK), :] = product[i * BLK : (i + 1) * BLK, j * BLK : (j + 1) * BLK]
                at += BLK
    sum_a = jnp.sum(scaled_a, axis=0, keepdims=True)
    sum_b = jnp.sum(scaled_b, axis=0, keepdims=True)
    for i in range(nb):
        out_ref[at + i : at + i + 1, :] = sum_a[:, i * BLK : (i + 1) * BLK]
        out_ref[at + nb + i : at + nb + i + 1, :] = sum_b[:, i * BLK : (i + 1) * BLK]
    total = jnp.sum(jnp.broadcast_to(weights, (weights.shape[0], BLK)), axis=0, keepdims=True)
    out_ref[at + 2 * nb : at + 2 * nb + 8, :] = jnp.broadcast_to(total, (8, BLK))


def invert_pair(one, two):
    size = one.shape[0]
    lane = lax.broadcasted_iota(jnp.int32, (size, size), 1)
    sub = lax.broadcasted_iota(jnp.int32, (size, size), 0)
    lane_row = lax.broadcasted_iota(jnp.int32, (1, size), 1)

    def step(m, k):
        column = m[:, k : k + 1]
        row = m[k : k + 1, :]
        inverse = 1.0 / m[k : k + 1, k : k + 1]
        row = jnp.where(lane_row == k, inverse, row * inverse)
        updated = jnp.where(lane == k, 0.0, m) - column * row
        return jnp.where(sub == k, row, updated)

    for k in range(size):
        one, two = step(one, k), step(two, k)
    return one, two


def solve_kernel(stats_ref, codes_ref, far_ref, weights_ref, score_ref, cot_a_ref, cot_b_ref, inv_ref, cross_ref):
    out = codes_ref.shape[1]
    nb = out // BLK
    tri = nb * (nb + 1) // 2
    base = (2 * tri + nb * nb) * BLK
    weight_sum = stats_ref[base + 2 * nb : base + 2 * nb + 1, 0:1]
    scale = 1.0 / weight_sum
    means_a = [stats_ref[base + i : base + i + 1, :] / weight_sum for i in range(nb)]
    means_b = [stats_ref[base + nb + i : base + nb + i + 1, :] / weight_sum for i in range(nb)]
    mean_a = jnp.concatenate(means_a, axis=1)
    mean_b = jnp.concatenate(means_b, axis=1)
    square = lax.broadcasted_iota(jnp.int32, (BLK, BLK), 0) == lax.broadcasted_iota(jnp.int32, (BLK, BLK), 1)
    ridge = jnp.where(square, EPS, 0.0)
    tall_a = [jnp.transpose(jnp.broadcast_to(m, (BLK, BLK))) for m in means_a]
    tall_b = [jnp.transpose(jnp.broadcast_to(m, (BLK, BLK))) for m in means_b]
    at = 0
    for which, tall, flat in ((0, tall_a, means_a), (1, tall_b, means_b)):
        for i in range(nb):
            for j in range(i, nb):
                block = stats_ref[pl.ds(at, BLK), :] / weight_sum - tall[i] * flat[j]
                if i == j:
                    block = block + ridge
                else:
                    inv_ref[which, j * BLK : (j + 1) * BLK, i * BLK : (i + 1) * BLK] = jnp.transpose(block)
                inv_ref[which, i * BLK : (i + 1) * BLK, j * BLK : (j + 1) * BLK] = block
                at += BLK
    for i in range(nb):
        for j in range(nb):
            cross_ref[i * BLK : (i + 1) * BLK, j * BLK : (j + 1) * BLK] = (
                stats_ref[pl.ds(at, BLK), :] / weight_sum - tall_a[i] * means_b[j]
            )
            at += BLK

    def pivot(block, _):
        here = pl.ds(pl.multiple_of(block * BLK, BLK), BLK)
        inverses = invert_pair(inv_ref[0, here, here], inv_ref[1, here, here])
        for which in range(2):
            panel = inv_ref[which, :, here]
            inv_ref[which, :, here] = jnp.zeros_like(panel)
            inv_ref[which, here, here] = jnp.zeros((BLK, BLK), jnp.float32)
            rows = mm(inverses[which], inv_ref[which, here, :])
            inv_ref[which, here, :] = rows
            inv_ref[which, here, here] = inverses[which]
            rows = inv_ref[which, here, :]
            inv_ref[which] = inv_ref[which] - mm(panel, rows)
            inv_ref[which, here, :] = rows
        return 0

    lax.fori_loop(0, nb, pivot, 0)
    inv_a, inv_b, cross = split(inv_ref[0]), split(inv_ref[1]), split(cross_ref[...])
    pull_a = mm3(inv_a, cross)
    pull_b = mm3(inv_b, cross, ((1,), (1,)))
    pull_a_parts = split(pull_a)
    middle = mm3(pull_a_parts, inv_b)
    score_ref[...] = jnp.sum(middle * cross_ref[...], axis=0, keepdims=True) / out
    middle = split(middle)
    codes = codes_ref[...]
    lagged = jnp.concatenate([codes[LAG:], far_ref[...].astype(jnp.float32)], axis=0)
    codes = codes - mean_a
    lagged = lagged - mean_b
    factor = weights_ref[...] * (2.0 / out * scale)
    rest_b = split(lagged - mm3(split(codes), pull_a_parts))
    cot_a_ref[...] = (factor * mm3(rest_b, middle, ((1,), (1,)))).astype(jnp.bfloat16)
    rest_a = split(codes - mm3(split(lagged), split(pull_b)))
    cot_b_ref[...] = (factor * mm3(rest_a, middle)).astype(jnp.bfloat16)


def backward_kernel(
    pattern_ref, frames_ref, second_ref, squash_ref, hidden_ref, cot_a_ref, cot_b_ref, back_ref, first_ref, grad_ref, pre_ref
):
    cols, slots = pattern_ref.shape
    depth = slots * BLK
    rows = cot_b_ref.shape[0]
    shifted = jnp.concatenate([back_ref[...], cot_b_ref[: rows - LAG, :]], axis=0)
    cotan = (cot_a_ref[...].astype(jnp.float32) + shifted.astype(jnp.float32)).astype(jnp.bfloat16)
    grad_ref[...] = mm_bf16(hidden_ref[...], cotan, ((0,), (0,)))
    squash = squash_ref[...]
    pre_ref[...] = (mm_bf16(cotan, second_ref[...], ((1,), (1,))) * (1.0 - squash * squash)).astype(jnp.bfloat16)

    def column(col, _):
        picked = picked_columns(pattern_ref, frames_ref, col, slots)
        back = pre_ref[:, pl.ds(pl.multiple_of(col * BLK, BLK), BLK)]
        first_ref[pl.ds(pl.multiple_of(col * depth, depth), depth), :] = mm_bf16(picked, back, ((0,), (0,)))
        return 0

    lax.fori_loop(0, cols, column, 0)


def call(kernel, shapes, specs, scratch=()):
    return pl.pallas_call(
        kernel,
        out_shape=[jax.ShapeDtypeStruct(s, d) for s, d in shapes],
        in_specs=specs,
        out_specs=[VMEM] * len(shapes),
        scratch_shapes=list(scratch),
        compiler_params=pltpu.CompilerParams(vmem_limit_bytes=LIMIT),
    )


def body(lengths, pattern, first_blocks, second_weight, frames, frame_ok):
    f32, bf16 = jnp.float32, jnp.bfloat16
    rows = frames.shape[0]
    hid, out = second_weight.shape
    nb = out // BLK
    offset = lax.axis_index("traj") * rows
    squash, hidden, codes = call(
        encode_kernel, [((rows, hid), f32), ((rows, hid), bf16), ((rows, out), f32)], [SMEM, VMEM, VMEM, VMEM]
    )(pattern, frames, first_blocks, second_weight)
    far_flags = from_behind(frame_ok[:LAG].astype(bf16), "traj", -1).astype(f32)
    far_codes = from_behind(codes[:LAG].astype(bf16), "traj", -1)
    ok_lagged = jnp.concatenate([frame_ok[LAG:].astype(f32), far_flags], axis=0)
    weights = pair_weights(lengths, frame_ok, ok_lagged, offset)[:, None]
    stat_rows = (nb * (nb + 1) + nb * nb) * BLK + 2 * nb + 8
    (local_stats,) = call(moments_kernel, [((stat_rows, BLK), f32)], [VMEM] * 3)(codes, far_codes, weights)
    stats = lax.psum(local_stats, "traj")
    score, cot_a, cot_b = call(
        solve_kernel,
        [((1, out), f32), ((rows, out), bf16), ((rows, out), bf16)],
        [VMEM] * 4,
        [pltpu.VMEM((2, out, out), f32), pltpu.VMEM((out, out), f32)],
    )(stats, codes, far_codes, weights)
    returned = from_behind(cot_b[rows - LAG :], "traj", 1)
    grad_first, grad_second = call(
        backward_kernel,
        [(first_blocks.shape, f32), ((hid, out), f32)],
        [SMEM] + [VMEM] * 7,
        [pltpu.VMEM((rows, hid), bf16)],
    )(pattern, frames, second_weight, squash, hidden, cot_a, cot_b, returned)
    share_first = lax.psum_scatter(grad_first, "traj", scatter_dimension=0, tiled=True)
    share_second = lax.psum_scatter(grad_second, "traj", scatter_dimension=0, tiled=True)
    return (jnp.sum(score).reshape(1), share_first, share_second)


def solution(mesh):
    placed = (P("groups"), P(), P(), P(), P(("groups", "traj"), None), P(("groups", "traj")))
    return jax.shard_map(
        body,
        mesh=mesh,
        in_specs=placed,
        out_specs=(P("groups"), P(("groups", "traj"), None), P(("groups", "traj"), None)),
        check_vma=False,
    )
```

```python
import functools

import jax
import jax.numpy as jnp
from jax import lax
from jax.experimental import pallas as pl
from jax.experimental.pallas import tpu as pltpu
from jax.sharding import PartitionSpec as P

BLK = 128
LAG = 64
EPS = 0.01
HIGHEST = lax.Precision.HIGHEST
VMEM = pl.BlockSpec(memory_space=pltpu.VMEM)
SMEM = pl.BlockSpec(memory_space=pltpu.SMEM)
LIMIT = 50 * 1024 * 1024


def from_behind(block, axis, distance):
    devices = range(lax.axis_size(axis))
    route = [(i - distance, i) for i in devices if i - distance in devices]
    return lax.ppermute(block, axis, route)


def pair_weights(lengths, ok_now, ok_lagged, offset):
    positions = offset + jnp.arange(ok_now.shape[0], dtype=jnp.int32)
    bounds = jnp.cumsum(lengths)
    owner_now = jnp.sum((bounds[None, :] <= positions[:, None]).astype(jnp.int32), axis=1)
    owner_lag = jnp.sum((bounds[None, :] <= (positions + LAG)[:, None]).astype(jnp.int32), axis=1)
    keep = (owner_now == owner_lag) & (ok_now > 0.5) & (ok_lagged > 0.5)
    return keep.astype(jnp.float32)


def mm(a, b, dims=((1,), (0,)), precision=HIGHEST):
    return lax.dot_general(
        a, b, (dims, ((), ())), precision=precision, preferred_element_type=jnp.float32
    )


def mm_bf16(a, b, dims=((1,), (0,))):
    return lax.dot_general(a, b, (dims, ((), ())), preferred_element_type=jnp.float32)


def split(x):
    high = x.astype(jnp.bfloat16)
    return high, (x - high.astype(jnp.float32)).astype(jnp.bfloat16)


def mm3(a, b, dims=((1,), (0,))):
    return mm_bf16(a[0], b[0], dims) + (mm_bf16(a[0], b[1], dims) + mm_bf16(a[1], b[0], dims))


def picked_columns(pattern_ref, frames_ref, col, slots):
    parts = []
    for slot in range(slots):
        start = pl.multiple_of(pattern_ref[col, slot] * BLK, BLK)
        parts.append(frames_ref[:, pl.ds(start, BLK)])
    return jnp.concatenate(parts, axis=1)


def encode_kernel(pattern_ref, frames_ref, first_ref, second_ref, squash_ref, hidden_ref, codes_ref):
    cols, slots = pattern_ref.shape
    depth = slots * BLK

    def column(col, _):
        picked = picked_columns(pattern_ref, frames_ref, col, slots)
        blocks = first_ref[pl.ds(pl.multiple_of(col * depth, depth), depth), :]
        squash = jnp.tanh(mm_bf16(picked, blocks))
        at = pl.ds(pl.multiple_of(col * BLK, BLK), BLK)
        squash_ref[:, at] = squash
        hidden_ref[:, at] = squash.astype(jnp.bfloat16)
        return 0

    lax.fori_loop(0, cols, column, 0)
    codes_ref[...] = mm_bf16(hidden_ref[...], second_ref[...])


def moments_kernel(codes_ref, far_ref, weights_ref, out_ref):
    codes = codes_ref[...]
    lagged = jnp.concatenate([codes[LAG:], far_ref[...].astype(jnp.float32)], axis=0)
    weights = weights_ref[...]
    scaled_a = codes * weights
    scaled_b = lagged * weights
    out = codes.shape[1]
    nb = out // BLK
    over_rows = ((0,), (0,))
    at = 0
    for left, right, whole in ((scaled_a, codes, False), (scaled_b, lagged, False), (scaled_a, lagged, True)):
        product = mm(left, right, over_rows)
        for i in range(nb):
            for j in range(0 if whole else i, nb):
                out_ref[pl.ds(at, BLK), :] = product[i * BLK : (i + 1) * BLK, j * BLK : (j + 1) * BLK]
                at += BLK
    sum_a = jnp.sum(scaled_a, axis=0, keepdims=True)
    sum_b = jnp.sum(scaled_b, axis=0, keepdims=True)
    for i in range(nb):
        out_ref[at + i : at + i + 1, :] = sum_a[:, i * BLK : (i + 1) * BLK]
        out_ref[at + nb + i : at + nb + i + 1, :] = sum_b[:, i * BLK : (i + 1) * BLK]
    total = jnp.sum(jnp.broadcast_to(weights, (weights.shape[0], BLK)), axis=0, keepdims=True)
    spare = out_ref.shape[0] - at - 2 * nb
    out_ref[at + 2 * nb :, :] = jnp.broadcast_to(total, (spare, BLK))


def invert_pair(one, two):
    size = one.shape[0]
    lane = lax.broadcasted_iota(jnp.int32, (size, size), 1)
    sub = lax.broadcasted_iota(jnp.int32, (size, size), 0)
    lane_row = lax.broadcasted_iota(jnp.int32, (1, size), 1)

    def step(m, k):
        column = m[:, k : k + 1]
        row = m[k : k + 1, :]
        inverse = 1.0 / m[k : k + 1, k : k + 1]
        row = jnp.where(lane_row == k, inverse, row * inverse)
        updated = jnp.where(lane == k, 0.0, m) - column * row
        return jnp.where(sub == k, row, updated)

    for k in range(size):
        one, two = step(one, k), step(two, k)
    return one, two


def solve_kernel(stats_ref, codes_ref, far_ref, weights_ref, score_ref, cot_a_ref, cot_b_ref, inv_ref, cross_ref):
    out = codes_ref.shape[1]
    nb = out // BLK
    tri = nb * (nb + 1) // 2
    base = (2 * tri + nb * nb) * BLK
    weight_sum = stats_ref[base + 2 * nb : base + 2 * nb + 1, 0:1]
    scale = 1.0 / weight_sum
    means_a = [stats_ref[base + i : base + i + 1, :] / weight_sum for i in range(nb)]
    means_b = [stats_ref[base + nb + i : base + nb + i + 1, :] / weight_sum for i in range(nb)]
    mean_a = jnp.concatenate(means_a, axis=1)
    mean_b = jnp.concatenate(means_b, axis=1)
    square = lax.broadcasted_iota(jnp.int32, (BLK, BLK), 0) == lax.broadcasted_iota(jnp.int32, (BLK, BLK), 1)
    ridge = jnp.where(square, EPS, 0.0)
    tall_a = [jnp.transpose(jnp.broadcast_to(m, (BLK, BLK))) for m in means_a]
    tall_b = [jnp.transpose(jnp.broadcast_to(m, (BLK, BLK))) for m in means_b]
    at = 0
    for which, tall, flat in ((0, tall_a, means_a), (1, tall_b, means_b)):
        for i in range(nb):
            for j in range(i, nb):
                block = stats_ref[pl.ds(at, BLK), :] / weight_sum - tall[i] * flat[j]
                if i == j:
                    block = block + ridge
                else:
                    inv_ref[which, j * BLK : (j + 1) * BLK, i * BLK : (i + 1) * BLK] = jnp.transpose(block)
                inv_ref[which, i * BLK : (i + 1) * BLK, j * BLK : (j + 1) * BLK] = block
                at += BLK
    for i in range(nb):
        for j in range(nb):
            cross_ref[i * BLK : (i + 1) * BLK, j * BLK : (j + 1) * BLK] = (
                stats_ref[pl.ds(at, BLK), :] / weight_sum - tall_a[i] * means_b[j]
            )
            at += BLK

    def pivot(block, _):
        here = pl.ds(pl.multiple_of(block * BLK, BLK), BLK)
        inverses = invert_pair(inv_ref[0, here, here], inv_ref[1, here, here])
        for which in range(2):
            panel = inv_ref[which, :, here]
            inv_ref[which, :, here] = jnp.zeros_like(panel)
            inv_ref[which, here, here] = jnp.zeros((BLK, BLK), jnp.float32)
            rows = mm(inverses[which], inv_ref[which, here, :])
            inv_ref[which, here, :] = rows
            inv_ref[which, here, here] = inverses[which]
            rows = inv_ref[which, here, :]
            inv_ref[which] = inv_ref[which] - mm(panel, rows)
            inv_ref[which, here, :] = rows
        return 0

    lax.fori_loop(0, nb, pivot, 0)
    inv_a, inv_b, cross = split(inv_ref[0]), split(inv_ref[1]), split(cross_ref[...])
    pull_a = mm3(inv_a, cross)
    pull_b = mm3(inv_b, cross, ((1,), (1,)))
    pull_a_parts = split(pull_a)
    middle = mm3(pull_a_parts, inv_b)
    score_ref[...] = jnp.sum(middle * cross_ref[...], axis=0, keepdims=True) / out
    middle = split(middle)
    codes = codes_ref[...]
    lagged = jnp.concatenate([codes[LAG:], far_ref[...].astype(jnp.float32)], axis=0)
    codes = codes - mean_a
    lagged = lagged - mean_b
    factor = weights_ref[...] * (2.0 / out * scale)
    rest_b = split(lagged - mm3(split(codes), pull_a_parts))
    cot_a_ref[...] = (factor * mm3(rest_b, middle, ((1,), (1,)))).astype(jnp.bfloat16)
    rest_a = split(codes - mm3(split(lagged), split(pull_b)))
    cot_b_ref[...] = (factor * mm3(rest_a, middle)).astype(jnp.bfloat16)


def backward_kernel(
    pattern_ref, frames_ref, second_ref, squash_ref, hidden_ref, cot_a_ref, cot_b_ref, back_ref, out_ref, pre_ref
):
    cols, slots = pattern_ref.shape
    depth = slots * BLK
    rows = cot_b_ref.shape[0]
    shifted = jnp.concatenate([back_ref[...], cot_b_ref[: rows - LAG, :]], axis=0)
    cotan = (cot_a_ref[...].astype(jnp.float32) + shifted.astype(jnp.float32)).astype(jnp.bfloat16)
    owners = out_ref.shape[0]
    top = cols * depth // owners
    tall = hidden_ref.shape[1] // owners
    grad = mm_bf16(hidden_ref[...], cotan, ((0,), (0,)))
    for i in range(grad.shape[1] // BLK):
        piece = grad[:, i * BLK : (i + 1) * BLK].reshape(owners, tall, BLK)
        out_ref[:, top + i * tall : top + (i + 1) * tall, :] = piece
    squash = squash_ref[...]
    pre_ref[...] = (mm_bf16(cotan, second_ref[...], ((1,), (1,))) * (1.0 - squash * squash)).astype(jnp.bfloat16)

    def column(col, _):
        picked = picked_columns(pattern_ref, frames_ref, col, slots)
        back = pre_ref[:, pl.ds(pl.multiple_of(col * BLK, BLK), BLK)]
        share = mm_bf16(picked, back, ((0,), (0,))).reshape(depth // top, top, BLK)
        out_ref[pl.ds(col * (depth // top), depth // top), :top, :] = share
        return 0

    lax.fori_loop(0, cols, column, 0)


def bit_orders(devices):
    bits = devices.bit_length() - 1
    turn = 1 + (bits - 1) // 2
    return list(range(bits)), [0] + list(range(turn, bits)) + list(range(1, turn))


def stage_shapes(devices, order):
    left = list(range(devices.bit_length() - 1))
    shapes = []
    for bit in order:
        place = left.index(bit)
        shapes.append((2 ** (len(left) - 1 - place), 2**place))
        left.remove(bit)
    return shapes


class Exchange:
    def __init__(self, devices, order, lo, rows, wire):
        self.order, self.shapes = order, stage_shapes(devices, order)
        self.lo, self.rows, self.wire = lo, rows, wire

    def scratch(self, gather):
        wide = [(hi, 2, low, self.rows, BLK) for hi, low in self.shapes]
        half = [(hi, low, self.rows, BLK) for hi, low in self.shapes]
        count = len(self.order)
        out = [pltpu.VMEM(s, jnp.float32) for s in wide[1:]]
        out += [pltpu.VMEM(s, self.wire) for s in half]
        out += [pltpu.VMEM(s, self.wire) for s in half]
        if gather:
            out += [pltpu.VMEM(s, jnp.float32) for s in wide]
        return out + [pltpu.SemaphoreType.DMA((2 * count,)), pltpu.SemaphoreType.DMA((2 * count,))]

    def bind(self, x_ref, refs, gather, me):
        count = len(self.order)
        self.x_ref, self.me = x_ref, me
        self.acc, refs = [None] + list(refs[: count - 1]), refs[count - 1 :]
        self.send, refs = refs[:count], refs[count:]
        self.recv, refs = refs[:count], refs[count:]
        if gather:
            self.full, refs = refs[:count], refs[count:]
        self.send_sem, self.recv_sem = refs
        self.bits = [(me // 2**b) % 2 for b in self.order]
        self.partners = [me + (1 - 2 * bit) * 2**b for bit, b in zip(self.bits, self.order)]
        self.copies = {}

    def part(self, stage, which):
        if stage == 0:
            hi, low = self.shapes[0]
            got = self.x_ref[:, which, self.lo : self.lo + self.rows, :]
            return got.reshape(hi, low, self.rows, BLK)
        return self.acc[stage][:, which]

    def copy(self, key, stage, src, dst):
        copy = pltpu.make_async_remote_copy(
            src_ref=src,
            dst_ref=dst,
            send_sem=self.send_sem.at[key],
            recv_sem=self.recv_sem.at[key],
            device_id={"traj": self.partners[stage]},
            device_id_type=pl.DeviceIdType.MESH,
        )
        copy.start()
        self.copies[key] = copy

    def start(self, stage):
        self.send[stage][...] = self.part(stage, 1 - self.bits[stage]).astype(self.wire)
        self.copy(stage, stage, self.send[stage], self.recv[stage])

    def finish(self, stage):
        self.copies[stage].wait()
        total = self.part(stage, self.bits[stage]) + self.recv[stage][...].astype(jnp.float32)
        if stage + 1 < len(self.order):
            self.acc[stage + 1][...] = total.reshape(self.acc[stage + 1].shape)
            return None
        return total

    def start_gather(self, stage, mine):
        hi, low = self.shapes[stage]
        bit = self.bits[stage]
        self.full[stage][:, bit] = mine.reshape(hi, low, self.rows, BLK)
        place = self.full[stage].at[:, bit]
        self.copy(len(self.order) + stage, stage, place, place)

    def finish_gather(self, stage):
        self.copies[len(self.order) + stage].wait()
        return self.full[stage][...]


def greet(partners):
    barrier = pltpu.get_barrier_semaphore()
    for partner in partners:
        pl.semaphore_signal(
            barrier, inc=1, device_id={"traj": partner}, device_id_type=pl.DeviceIdType.MESH
        )
    pl.semaphore_wait(barrier, len(partners))


def run_halving(exchanges):
    stages = len(exchanges[0].order)
    for stage in range(stages):
        for ex in exchanges:
            if stage > 0:
                ex.finish(stage - 1)
            ex.start(stage)
    return [ex.finish(stages - 1) for ex in exchanges]


def bind_all(exchanges, x_ref, refs, gather):
    me = lax.axis_index("traj")
    for ex in exchanges:
        count = len(ex.scratch(gather))
        ex.bind(x_ref, refs[:count], gather, me)
        refs = refs[count:]
    greet(exchanges[0].partners)


def reduce_kernel(exchanges, x_ref, out_ref, *refs):
    bind_all(exchanges, x_ref, refs, True)
    mine = run_halving(exchanges)
    stages = len(exchanges[0].order)
    for stage in reversed(range(stages)):
        for i, ex in enumerate(exchanges):
            if stage + 1 < stages:
                mine[i] = ex.finish_gather(stage + 1)
            ex.start_gather(stage, mine[i])
    for ex in exchanges:
        whole = ex.finish_gather(0)
        out_ref[:, :, ex.lo : ex.lo + ex.rows, :] = whole.reshape(-1, 2, ex.rows, BLK)


def scatter_kernel(exchanges, x_ref, first_ref, second_ref, *refs):
    bind_all(exchanges, x_ref, refs[1:], False)
    chunk_ref = refs[0]
    for ex, total in zip(exchanges, run_halving(exchanges)):
        chunk_ref[ex.lo : ex.lo + ex.rows, :] = total.reshape(ex.rows, BLK)
    top = first_ref.shape[0]
    first_ref[...] = chunk_ref[:top, :]
    tall, wide = second_ref.shape
    for i in range(wide // BLK):
        second_ref[:, i * BLK : (i + 1) * BLK] = chunk_ref[top + i * tall : top + (i + 1) * tall, :]


def exchanges_for(devices, rows, wire, align):
    head = -(-(rows // 2) // align) * align
    one, two = bit_orders(devices)
    return [Exchange(devices, one, 0, head, wire), Exchange(devices, two, head, rows - head, wire)]


def exchange_call(kernel, exchanges, shapes, gather, ident, extra=()):
    scratch = list(extra) + [s for ex in exchanges for s in ex.scratch(gather)]
    return pl.pallas_call(
        functools.partial(kernel, exchanges),
        out_shape=[jax.ShapeDtypeStruct(s, jnp.float32) for s in shapes],
        in_specs=[VMEM],
        out_specs=[VMEM] * len(shapes),
        scratch_shapes=scratch,
        compiler_params=pltpu.CompilerParams(
            collective_id=ident, has_side_effects=True, vmem_limit_bytes=LIMIT
        ),
    )


def call(kernel, shapes, specs, scratch=()):
    return pl.pallas_call(
        kernel,
        out_shape=[jax.ShapeDtypeStruct(s, d) for s, d in shapes],
        in_specs=specs,
        out_specs=[VMEM] * len(shapes),
        scratch_shapes=list(scratch),
        compiler_params=pltpu.CompilerParams(vmem_limit_bytes=LIMIT),
    )


def body(lengths, pattern, first_blocks, second_weight, frames, frame_ok):
    f32, bf16 = jnp.float32, jnp.bfloat16
    rows = frames.shape[0]
    hid, out = second_weight.shape
    nb = out // BLK
    offset = lax.axis_index("traj") * rows
    squash, hidden, codes = call(
        encode_kernel, [((rows, hid), f32), ((rows, hid), bf16), ((rows, out), f32)], [SMEM, VMEM, VMEM, VMEM]
    )(pattern, frames, first_blocks, second_weight)
    far_flags = from_behind(frame_ok[:LAG].astype(bf16), "traj", -1).astype(f32)
    far_codes = from_behind(codes[:LAG].astype(bf16), "traj", -1)
    ok_lagged = jnp.concatenate([frame_ok[LAG:].astype(f32), far_flags], axis=0)
    weights = pair_weights(lengths, frame_ok, ok_lagged, offset)[:, None]
    devices = lax.axis_size("traj")
    used = (nb * (nb + 1) + nb * nb) * BLK + 2 * nb + 8
    per = -(-used // (8 * devices)) * 8
    (local_stats,) = call(moments_kernel, [((devices * per, BLK), f32)], [VMEM] * 3)(codes, far_codes, weights)
    halves = (devices // 2, 2, per, BLK)
    (stats,) = exchange_call(reduce_kernel, exchanges_for(devices, per, f32, 8), [halves], True, 0)(
        local_stats.reshape(halves)
    )
    stats = stats.reshape(devices * per, BLK)
    score, cot_a, cot_b = call(
        solve_kernel,
        [((1, out), f32), ((rows, out), bf16), ((rows, out), bf16)],
        [VMEM] * 4,
        [pltpu.VMEM((2, out, out), f32), pltpu.VMEM((out, out), f32)],
    )(stats, codes, far_codes, weights)
    returned = from_behind(cot_b[rows - LAG :], "traj", 1)
    top, tall = first_blocks.shape[0] // devices, hid // devices
    chunk = top + tall * nb
    (grads,) = call(
        backward_kernel, [((devices, chunk, BLK), f32)], [SMEM] + [VMEM] * 7, [pltpu.VMEM((rows, hid), bf16)]
    )(pattern, frames, second_weight, squash, hidden, cot_a, cot_b, returned)
    share_first, share_second = exchange_call(
        scatter_kernel,
        exchanges_for(devices, chunk, bf16, 16),
        [(top, BLK), (tall, out)],
        False,
        1,
        [pltpu.VMEM((chunk, BLK), f32)],
    )(grads.reshape(devices // 2, 2, chunk, BLK))
    return (jnp.sum(score).reshape(1), share_first, share_second)


def solution(mesh):
    placed = (P("groups"), P(), P(), P(), P(("groups", "traj"), None), P(("groups", "traj")))
    return jax.shard_map(
        body,
        mesh=mesh,
        in_specs=placed,
        out_specs=(P("groups"), P(("groups", "traj"), None), P(("groups", "traj"), None)),
        check_vma=False,
    )
```

```python
import functools

import jax
import jax.numpy as jnp
from jax import lax
from jax.experimental import pallas as pl
from jax.experimental.pallas import tpu as pltpu
from jax.sharding import PartitionSpec as P

BLK = 128
LAG = 64
EPS = 0.01
PIVOTS = 4
HIGHEST = lax.Precision.HIGHEST
VMEM = pl.BlockSpec(memory_space=pltpu.VMEM)
SMEM = pl.BlockSpec(memory_space=pltpu.SMEM)
LIMIT = 50 * 1024 * 1024


def from_behind(block, axis, distance):
    devices = range(lax.axis_size(axis))
    route = [(i - distance, i) for i in devices if i - distance in devices]
    return lax.ppermute(block, axis, route)


def pair_weights(lengths, ok_now, ok_lagged, offset):
    positions = offset + jnp.arange(ok_now.shape[0], dtype=jnp.int32)
    bounds = jnp.cumsum(lengths)
    owner_now = jnp.sum((bounds[None, :] <= positions[:, None]).astype(jnp.int32), axis=1)
    owner_lag = jnp.sum((bounds[None, :] <= (positions + LAG)[:, None]).astype(jnp.int32), axis=1)
    keep = (owner_now == owner_lag) & (ok_now > 0.5) & (ok_lagged > 0.5)
    return keep.astype(jnp.float32)


def mm(a, b, dims=((1,), (0,)), precision=HIGHEST):
    return lax.dot_general(
        a, b, (dims, ((), ())), precision=precision, preferred_element_type=jnp.float32
    )


def mm_bf16(a, b, dims=((1,), (0,))):
    return lax.dot_general(a, b, (dims, ((), ())), preferred_element_type=jnp.float32)


def split(x):
    high = x.astype(jnp.bfloat16)
    return high, (x - high.astype(jnp.float32)).astype(jnp.bfloat16)


def mm3(a, b, dims=((1,), (0,))):
    return mm_bf16(a[0], b[0], dims) + (mm_bf16(a[0], b[1], dims) + mm_bf16(a[1], b[0], dims))


def picked_columns(pattern_ref, frames_ref, col, slots):
    parts = []
    for slot in range(slots):
        start = pl.multiple_of(pattern_ref[col, slot] * BLK, BLK)
        parts.append(frames_ref[:, pl.ds(start, BLK)])
    return jnp.concatenate(parts, axis=1)


def encode_kernel(pattern_ref, frames_ref, first_ref, second_ref, squash_ref, hidden_ref, codes_ref):
    cols, slots = pattern_ref.shape
    depth = slots * BLK

    def column(col, _):
        picked = picked_columns(pattern_ref, frames_ref, col, slots)
        blocks = first_ref[pl.ds(pl.multiple_of(col * depth, depth), depth), :]
        squash = jnp.tanh(mm_bf16(picked, blocks))
        at = pl.ds(pl.multiple_of(col * BLK, BLK), BLK)
        squash_ref[:, at] = squash
        hidden_ref[:, at] = squash.astype(jnp.bfloat16)
        return 0

    lax.fori_loop(0, cols, column, 0)
    codes_ref[...] = mm_bf16(hidden_ref[...], second_ref[...])


def moments_kernel(codes_ref, far_ref, weights_ref, out_ref):
    codes = codes_ref[...]
    lagged = jnp.concatenate([codes[LAG:], far_ref[...].astype(jnp.float32)], axis=0)
    weights = weights_ref[...]
    scaled_a = codes * weights
    scaled_b = lagged * weights
    out = codes.shape[1]
    nb = out // BLK
    over_rows = ((0,), (0,))
    at = 0
    for left, right, whole in ((scaled_a, codes, False), (scaled_b, lagged, False), (scaled_a, lagged, True)):
        product = mm(left, right, over_rows)
        for i in range(nb):
            for j in range(0 if whole else i, nb):
                out_ref[pl.ds(at, BLK), :] = product[i * BLK : (i + 1) * BLK, j * BLK : (j + 1) * BLK]
                at += BLK
    sum_a = jnp.sum(scaled_a, axis=0, keepdims=True)
    sum_b = jnp.sum(scaled_b, axis=0, keepdims=True)
    for i in range(nb):
        out_ref[at + i : at + i + 1, :] = sum_a[:, i * BLK : (i + 1) * BLK]
        out_ref[at + nb + i : at + nb + i + 1, :] = sum_b[:, i * BLK : (i + 1) * BLK]
    total = jnp.sum(jnp.broadcast_to(weights, (weights.shape[0], BLK)), axis=0, keepdims=True)
    spare = out_ref.shape[0] - at - 2 * nb
    out_ref[at + 2 * nb :, :] = jnp.broadcast_to(total, (spare, BLK))


def eliminate(tiles, first, count):
    lane = lax.broadcasted_iota(jnp.int32, (8, BLK), 1)
    sub = lax.broadcasted_iota(jnp.int32, (8, BLK), 0)
    span = range(count)
    home, top = first // 8, first % 8
    wide = lambda x: jnp.broadcast_to(x, (8, BLK))
    rows = [wide(tiles[home][top + i : top + i + 1, :]) for i in span]
    inv = [[wide(rows[i][:, first + j : first + j + 1]) for j in span] for i in span]
    for k in span:
        scale = 1.0 / inv[k][k]
        row = [scale if j == k else inv[k][j] * scale for j in span]
        inv = [
            row if i == k else [-inv[i][k] * scale if j == k else inv[i][j] - inv[i][k] * row[j] for j in span]
            for i in span
        ]
    fresh = []
    for i in span:
        row = sum(inv[i][j] * rows[j] for j in span)
        for j in span:
            row = jnp.where(lane == first + j, inv[i][j], row)
        fresh.append(row)
    inside = (lane >= first) & (lane < first + count)
    out = []
    for tile in tiles:
        columns = [wide(tile[:, first + j : first + j + 1]) for j in span]
        out.append(jnp.where(inside, 0.0, tile) - sum(columns[j] * fresh[j] for j in span))
    for i in span:
        out[home] = jnp.where(sub == top + i, fresh[i], out[home])
    return out


def invert_pair(one, two):
    one, two = [[m[i : i + 8, :] for i in range(0, BLK, 8)] for m in (one, two)]
    for first in range(0, BLK, PIVOTS):
        one, two = eliminate(one, first, PIVOTS), eliminate(two, first, PIVOTS)
    return jnp.concatenate(one, axis=0), jnp.concatenate(two, axis=0)


def solve_kernel(stats_ref, codes_ref, far_ref, weights_ref, score_ref, cot_a_ref, cot_b_ref, inv_ref, cross_ref):
    out = codes_ref.shape[1]
    nb = out // BLK
    tri = nb * (nb + 1) // 2
    base = (2 * tri + nb * nb) * BLK
    weight_sum = stats_ref[base + 2 * nb : base + 2 * nb + 1, 0:1]
    scale = 1.0 / weight_sum
    means_a = [stats_ref[base + i : base + i + 1, :] / weight_sum for i in range(nb)]
    means_b = [stats_ref[base + nb + i : base + nb + i + 1, :] / weight_sum for i in range(nb)]
    mean_a = jnp.concatenate(means_a, axis=1)
    mean_b = jnp.concatenate(means_b, axis=1)
    square = lax.broadcasted_iota(jnp.int32, (BLK, BLK), 0) == lax.broadcasted_iota(jnp.int32, (BLK, BLK), 1)
    ridge = jnp.where(square, EPS, 0.0)
    tall_a = [jnp.transpose(jnp.broadcast_to(m, (BLK, BLK))) for m in means_a]
    tall_b = [jnp.transpose(jnp.broadcast_to(m, (BLK, BLK))) for m in means_b]
    at = 0
    for which, tall, flat in ((0, tall_a, means_a), (1, tall_b, means_b)):
        for i in range(nb):
            for j in range(i, nb):
                block = stats_ref[pl.ds(at, BLK), :] / weight_sum - tall[i] * flat[j]
                if i == j:
                    block = block + ridge
                else:
                    inv_ref[which, j * BLK : (j + 1) * BLK, i * BLK : (i + 1) * BLK] = jnp.transpose(block)
                inv_ref[which, i * BLK : (i + 1) * BLK, j * BLK : (j + 1) * BLK] = block
                at += BLK
    for i in range(nb):
        for j in range(nb):
            cross_ref[i * BLK : (i + 1) * BLK, j * BLK : (j + 1) * BLK] = (
                stats_ref[pl.ds(at, BLK), :] / weight_sum - tall_a[i] * means_b[j]
            )
            at += BLK

    def pivot(block, _):
        here = pl.ds(pl.multiple_of(block * BLK, BLK), BLK)
        inverses = invert_pair(inv_ref[0, here, here], inv_ref[1, here, here])
        for which in range(2):
            panel = inv_ref[which, :, here]
            inv_ref[which, :, here] = jnp.zeros_like(panel)
            inv_ref[which, here, here] = jnp.zeros((BLK, BLK), jnp.float32)
            rows = mm(inverses[which], inv_ref[which, here, :])
            inv_ref[which, here, :] = rows
            inv_ref[which, here, here] = inverses[which]
            rows = inv_ref[which, here, :]
            inv_ref[which] = inv_ref[which] - mm(panel, rows)
            inv_ref[which, here, :] = rows
        return 0

    lax.fori_loop(0, nb, pivot, 0)
    inv_a, inv_b, cross = split(inv_ref[0]), split(inv_ref[1]), split(cross_ref[...])
    pull_a = mm3(inv_a, cross)
    pull_b = mm3(inv_b, cross, ((1,), (1,)))
    pull_a_parts = split(pull_a)
    middle = mm3(pull_a_parts, inv_b)
    score_ref[...] = jnp.sum(middle * cross_ref[...], axis=0, keepdims=True) / out
    middle = split(middle)
    codes = codes_ref[...]
    lagged = jnp.concatenate([codes[LAG:], far_ref[...].astype(jnp.float32)], axis=0)
    codes = codes - mean_a
    lagged = lagged - mean_b
    factor = weights_ref[...] * (2.0 / out * scale)
    rest_b = split(lagged - mm3(split(codes), pull_a_parts))
    cot_a_ref[...] = (factor * mm3(rest_b, middle, ((1,), (1,)))).astype(jnp.bfloat16)
    rest_a = split(codes - mm3(split(lagged), split(pull_b)))
    cot_b_ref[...] = (factor * mm3(rest_a, middle)).astype(jnp.bfloat16)


def backward_kernel(
    pattern_ref, frames_ref, second_ref, squash_ref, hidden_ref, cot_a_ref, cot_b_ref, back_ref, out_ref, pre_ref
):
    cols, slots = pattern_ref.shape
    depth = slots * BLK
    rows = cot_b_ref.shape[0]
    shifted = jnp.concatenate([back_ref[...], cot_b_ref[: rows - LAG, :]], axis=0)
    cotan = (cot_a_ref[...].astype(jnp.float32) + shifted.astype(jnp.float32)).astype(jnp.bfloat16)
    owners = out_ref.shape[0]
    top = cols * depth // owners
    tall = hidden_ref.shape[1] // owners
    grad = mm_bf16(hidden_ref[...], cotan, ((0,), (0,)))
    for i in range(grad.shape[1] // BLK):
        piece = grad[:, i * BLK : (i + 1) * BLK].reshape(owners, tall, BLK)
        out_ref[:, top + i * tall : top + (i + 1) * tall, :] = piece
    squash = squash_ref[...]
    pre_ref[...] = (mm_bf16(cotan, second_ref[...], ((1,), (1,))) * (1.0 - squash * squash)).astype(jnp.bfloat16)

    def column(col, _):
        picked = picked_columns(pattern_ref, frames_ref, col, slots)
        back = pre_ref[:, pl.ds(pl.multiple_of(col * BLK, BLK), BLK)]
        share = mm_bf16(picked, back, ((0,), (0,))).reshape(depth // top, top, BLK)
        out_ref[pl.ds(col * (depth // top), depth // top), :top, :] = share
        return 0

    lax.fori_loop(0, cols, column, 0)


def bit_orders(devices):
    bits = devices.bit_length() - 1
    turn = 1 + (bits - 1) // 2
    return list(range(bits)), [0] + list(range(turn, bits)) + list(range(1, turn))


def stage_shapes(devices, order):
    left = list(range(devices.bit_length() - 1))
    shapes = []
    for bit in order:
        place = left.index(bit)
        shapes.append((2 ** (len(left) - 1 - place), 2**place))
        left.remove(bit)
    return shapes


class Exchange:
    def __init__(self, devices, order, lo, rows, wire):
        self.order, self.shapes = order, stage_shapes(devices, order)
        self.lo, self.rows, self.wire = lo, rows, wire

    def scratch(self, gather):
        wide = [(hi, 2, low, self.rows, BLK) for hi, low in self.shapes]
        half = [(hi, low, self.rows, BLK) for hi, low in self.shapes]
        count = len(self.order)
        out = [pltpu.VMEM(s, jnp.float32) for s in wide[1:]]
        out += [pltpu.VMEM(s, self.wire) for s in half]
        out += [pltpu.VMEM(s, self.wire) for s in half]
        if gather:
            out += [pltpu.VMEM(s, jnp.float32) for s in wide]
        return out + [pltpu.SemaphoreType.DMA((2 * count,)), pltpu.SemaphoreType.DMA((2 * count,))]

    def bind(self, x_ref, refs, gather, me):
        count = len(self.order)
        self.x_ref, self.me = x_ref, me
        self.acc, refs = [None] + list(refs[: count - 1]), refs[count - 1 :]
        self.send, refs = refs[:count], refs[count:]
        self.recv, refs = refs[:count], refs[count:]
        if gather:
            self.full, refs = refs[:count], refs[count:]
        self.send_sem, self.recv_sem = refs
        self.bits = [(me // 2**b) % 2 for b in self.order]
        self.partners = [me + (1 - 2 * bit) * 2**b for bit, b in zip(self.bits, self.order)]
        self.copies = {}

    def part(self, stage, which):
        if stage == 0:
            hi, low = self.shapes[0]
            got = self.x_ref[:, which, self.lo : self.lo + self.rows, :]
            return got.reshape(hi, low, self.rows, BLK)
        return self.acc[stage][:, which]

    def copy(self, key, stage, src, dst):
        copy = pltpu.make_async_remote_copy(
            src_ref=src,
            dst_ref=dst,
            send_sem=self.send_sem.at[key],
            recv_sem=self.recv_sem.at[key],
            device_id={"traj": self.partners[stage]},
            device_id_type=pl.DeviceIdType.MESH,
        )
        copy.start()
        self.copies[key] = copy

    def start(self, stage):
        self.send[stage][...] = self.part(stage, 1 - self.bits[stage]).astype(self.wire)
        self.copy(stage, stage, self.send[stage], self.recv[stage])

    def finish(self, stage):
        self.copies[stage].wait()
        total = self.part(stage, self.bits[stage]) + self.recv[stage][...].astype(jnp.float32)
        if stage + 1 < len(self.order):
            self.acc[stage + 1][...] = total.reshape(self.acc[stage + 1].shape)
            return None
        return total

    def start_gather(self, stage, mine):
        hi, low = self.shapes[stage]
        bit = self.bits[stage]
        self.full[stage][:, bit] = mine.reshape(hi, low, self.rows, BLK)
        place = self.full[stage].at[:, bit]
        self.copy(len(self.order) + stage, stage, place, place)

    def finish_gather(self, stage):
        self.copies[len(self.order) + stage].wait()
        return self.full[stage][...]


def greet(partners):
    barrier = pltpu.get_barrier_semaphore()
    for partner in partners:
        pl.semaphore_signal(
            barrier, inc=1, device_id={"traj": partner}, device_id_type=pl.DeviceIdType.MESH
        )
    pl.semaphore_wait(barrier, len(partners))


def run_halving(exchanges):
    stages = len(exchanges[0].order)
    for stage in range(stages):
        for ex in exchanges:
            if stage > 0:
                ex.finish(stage - 1)
            ex.start(stage)
    return [ex.finish(stages - 1) for ex in exchanges]


def bind_all(exchanges, x_ref, refs, gather):
    me = lax.axis_index("traj")
    for ex in exchanges:
        count = len(ex.scratch(gather))
        ex.bind(x_ref, refs[:count], gather, me)
        refs = refs[count:]
    greet(exchanges[0].partners)


def reduce_kernel(exchanges, x_ref, out_ref, *refs):
    bind_all(exchanges, x_ref, refs, True)
    mine = run_halving(exchanges)
    stages = len(exchanges[0].order)
    for stage in reversed(range(stages)):
        for i, ex in enumerate(exchanges):
            if stage + 1 < stages:
                mine[i] = ex.finish_gather(stage + 1)
            ex.start_gather(stage, mine[i])
    for ex in exchanges:
        whole = ex.finish_gather(0)
        out_ref[:, :, ex.lo : ex.lo + ex.rows, :] = whole.reshape(-1, 2, ex.rows, BLK)


def scatter_kernel(exchanges, x_ref, first_ref, second_ref, *refs):
    bind_all(exchanges, x_ref, refs[1:], False)
    chunk_ref = refs[0]
    for ex, total in zip(exchanges, run_halving(exchanges)):
        chunk_ref[ex.lo : ex.lo + ex.rows, :] = total.reshape(ex.rows, BLK)
    top = first_ref.shape[0]
    first_ref[...] = chunk_ref[:top, :]
    tall, wide = second_ref.shape
    for i in range(wide // BLK):
        second_ref[:, i * BLK : (i + 1) * BLK] = chunk_ref[top + i * tall : top + (i + 1) * tall, :]


def exchanges_for(devices, rows, wire, align, parts):
    orders = bit_orders(devices)
    units = rows // align
    parts = min(parts, units)
    ends = [align * (units * i // parts) for i in range(parts + 1)]
    return [
        Exchange(devices, orders[i % 2], ends[i], ends[i + 1] - ends[i], wire) for i in range(parts)
    ]


def exchange_call(kernel, exchanges, shapes, gather, ident, extra=()):
    scratch = list(extra) + [s for ex in exchanges for s in ex.scratch(gather)]
    return pl.pallas_call(
        functools.partial(kernel, exchanges),
        out_shape=[jax.ShapeDtypeStruct(s, jnp.float32) for s in shapes],
        in_specs=[VMEM],
        out_specs=[VMEM] * len(shapes),
        scratch_shapes=scratch,
        compiler_params=pltpu.CompilerParams(
            collective_id=ident, has_side_effects=True, vmem_limit_bytes=LIMIT
        ),
    )


def call(kernel, shapes, specs, scratch=()):
    return pl.pallas_call(
        kernel,
        out_shape=[jax.ShapeDtypeStruct(s, d) for s, d in shapes],
        in_specs=specs,
        out_specs=[VMEM] * len(shapes),
        scratch_shapes=list(scratch),
        compiler_params=pltpu.CompilerParams(vmem_limit_bytes=LIMIT),
    )


def body(lengths, pattern, first_blocks, second_weight, frames, frame_ok):
    f32, bf16 = jnp.float32, jnp.bfloat16
    rows = frames.shape[0]
    hid, out = second_weight.shape
    nb = out // BLK
    offset = lax.axis_index("traj") * rows
    squash, hidden, codes = call(
        encode_kernel, [((rows, hid), f32), ((rows, hid), bf16), ((rows, out), f32)], [SMEM, VMEM, VMEM, VMEM]
    )(pattern, frames, first_blocks, second_weight)
    far_flags = from_behind(frame_ok[:LAG].astype(bf16), "traj", -1).astype(f32)
    far_codes = from_behind(codes[:LAG].astype(bf16), "traj", -1)
    ok_lagged = jnp.concatenate([frame_ok[LAG:].astype(f32), far_flags], axis=0)
    weights = pair_weights(lengths, frame_ok, ok_lagged, offset)[:, None]
    devices = lax.axis_size("traj")
    used = (nb * (nb + 1) + nb * nb) * BLK + 2 * nb + 8
    per = -(-used // (8 * devices)) * 8
    (local_stats,) = call(moments_kernel, [((devices * per, BLK), f32)], [VMEM] * 3)(codes, far_codes, weights)
    halves = (devices // 2, 2, per, BLK)
    (stats,) = exchange_call(reduce_kernel, exchanges_for(devices, per, f32, 8, 4), [halves], True, 0)(
        local_stats.reshape(halves)
    )
    stats = stats.reshape(devices * per, BLK)
    score, cot_a, cot_b = call(
        solve_kernel,
        [((1, out), f32), ((rows, out), bf16), ((rows, out), bf16)],
        [VMEM] * 4,
        [pltpu.VMEM((2, out, out), f32), pltpu.VMEM((out, out), f32)],
    )(stats, codes, far_codes, weights)
    returned = from_behind(cot_b[rows - LAG :], "traj", 1)
    top, tall = first_blocks.shape[0] // devices, hid // devices
    chunk = top + tall * nb
    (grads,) = call(
        backward_kernel, [((devices, chunk, BLK), f32)], [SMEM] + [VMEM] * 7, [pltpu.VMEM((rows, hid), bf16)]
    )(pattern, frames, second_weight, squash, hidden, cot_a, cot_b, returned)
    share_first, share_second = exchange_call(
        scatter_kernel,
        exchanges_for(devices, chunk, bf16, 16, 4),
        [(top, BLK), (tall, out)],
        False,
        1,
        [pltpu.VMEM((chunk, BLK), f32)],
    )(grads.reshape(devices // 2, 2, chunk, BLK))
    return (jnp.sum(score).reshape(1), share_first, share_second)


def solution(mesh):
    placed = (P("groups"), P(), P(), P(), P(("groups", "traj"), None), P(("groups", "traj")))
    return jax.shard_map(
        body,
        mesh=mesh,
        in_specs=placed,
        out_specs=(P("groups"), P(("groups", "traj"), None), P(("groups", "traj"), None)),
        check_vma=False,
    )
```
